256 devices in a mesh: section: 32 (over z_lo, x, core), tensor: 8 (over z_hi, y).
Axes of the slice: x: 4, y: 4, z: 8 (z_hi: 2, z_lo: 4; z = z_hi * 4 + z_lo), core: 2. Of those that a mesh axis runs over, the one named last changes fastest.
Arguments:
- stream_two: bfloat16 [32, 128, 4096], P('section', None, 'tensor'), may hold values from -6 to 6
- block_last: bfloat16 [32, 128, 4096], P('section', None, 'tensor'), may hold values from -3 to 3
- incoming_two: bfloat16 [2, 128, 4096], P(None, None, 'tensor'), may hold values from -6 to 6
- incoming_last: bfloat16 [2, 128, 4096], P(None, None, 'tensor'), may hold values from -3 to 3
- norm_gain: bfloat16 [32, 4096], P('section'), may hold values from 0.099609375 to 1.8984375
- w_query: bfloat16 [32, 4096, 4096], P('section', None, 'tensor'), may hold values from -0.09375 to 0.09375
- w_keyval: bfloat16 [32, 4096, 2, 1024], P('section', None, None, 'tensor'), may hold values from -0.09375 to 0.09375
- w_out: bfloat16 [32, 4096, 4096], P('section', 'tensor'), may hold values from -0.09375 to 0.09375
- keys_cache: bfloat16 [32, 3, 512, 1024], P('section', None, None, 'tensor'), may hold values from -500 to 500, as said below
- values_cache: bfloat16 [32, 3, 512, 1024], P('section', None, None, 'tensor'), may hold values from -6 to 6
- cached_len: int32 [34], replicated, may hold values from 128 to 512, as said below
Outputs:
- stream_out: bfloat16 [32, 3, 128, 4096], P('section', None, None, 'tensor')
- block_out: bfloat16 [32, 3, 128, 4096], P('section', None, None, 'tensor')
The draws below stay inside these ranges and needn't reach their ends.
Inputs may be any that keep to these rules, and one draw needn't show every extreme that they name: `cached_len`: one micro-batch's length is 512 in every draw. `keys_cache`: keys already rotated to their positions.
All inputs are finite; a program needn't handle non-finite values.
Results may differ from the reference program's by a relative error of at most 0.025.
Values may be sent and summed in bfloat16 or wider, within the bound.
No kernel may reach another device: no remote copies, remote signals or barrier semaphores. Data moves between devices by JAX's collectives and lax.ppermute only.
A program may use at most 128 MiB of HBM per device.

```python
import jax
import jax.numpy as jnp
from jax import lax

D = 4096
HQ = 32
KVH = 8
HD = 128
TOK = 128
CTX = 512
TICKS = 3
LAYERS = 32
MICRO = 34
N_TENSOR = 8


def draw_keys_cache(key, part):
    key = jax.random.fold_in(key, 7)
    base = jax.random.normal(key, (LAYERS, TICKS, CTX, KVH * HD), jnp.float32)
    return jnp.clip(base, -500.0, 500.0).astype(jnp.bfloat16)


def draw_cached_len(key, part):
    key = jax.random.fold_in(key, 11)
    key_lengths, key_spot = jax.random.split(key)
    lengths = jax.random.randint(key_lengths, (MICRO,), CTX // 4, CTX + 1)
    spot = jax.random.randint(key_spot, (), 0, MICRO)
    return lengths.at[spot].set(CTX).astype(jnp.int32)


def level_of(key, dims, cuts, low, largest):
    gain = 1.0
    for dim, blocks in cuts:
        heights = jax.random.uniform(jax.random.fold_in(jax.random.fold_in(key, 6), dim), (blocks,), jnp.float32, low / len(cuts), largest / len(cuts))
        gain = gain * jnp.repeat(jnp.exp(heights), dims[dim] // blocks).reshape((-1,) + (1,) * (len(dims) - 1 - dim))
    return gain


def noise(key, extent, spread, bound, cuts=(), held_as=jnp.bfloat16):
    level = level_of(key, extent, cuts, -0.22, 0.18) if cuts else 1.0
    result = jax.random.normal(key, extent, jnp.float32) * spread * level
    return jnp.minimum(jnp.maximum(result, -bound), bound).astype(held_as)


def setup_inputs(seed: int = 0) -> dict:
    arg_keys = jax.random.split(jax.random.key(seed), 12)
    stream_two = noise(arg_keys[0], (LAYERS, TOK, D), 1.0, 6.0, ((0, 32), (2, 8)))
    block_last = noise(arg_keys[1], (LAYERS, TOK, D), 0.5, 3.0, ((0, 32), (2, 8)))
    incoming_two = noise(arg_keys[2], (TICKS - 1, TOK, D), 1.0, 6.0, ((2, 8),))
    incoming_last = noise(arg_keys[3], (TICKS - 1, TOK, D), 0.5, 3.0, ((2, 8),))
    norm_gain = jnp.clip(1.0 + 0.18 * jax.random.normal(arg_keys[4], (LAYERS, D), jnp.float32), 0.099609375, 1.8984375).astype(jnp.bfloat16)
    w_query = noise(arg_keys[5], (LAYERS, D, HQ * HD), D ** -0.5, 0.09375, ((0, 32), (2, 8)))
    w_keyval = noise(arg_keys[6], (LAYERS, D, 2, KVH * HD), D ** -0.5, 0.09375, ((0, 32), (3, 8)))
    w_out = noise(arg_keys[7], (LAYERS, HQ * HD, D), (HQ * HD) ** -0.5, 0.09375, ((0, 32), (1, 8)))
    keys_cache = draw_keys_cache(jax.random.fold_in(arg_keys[11], 71), 0)
    values_cache = noise(arg_keys[9], (LAYERS, TICKS, CTX, KVH * HD), 1.0, 6.0, ((0, 32), (3, 8)))
    cached_len = draw_cached_len(jax.random.fold_in(arg_keys[11], 71), 0)
    return dict(stream_two=stream_two, block_last=block_last, incoming_two=incoming_two, incoming_last=incoming_last, norm_gain=norm_gain, w_query=w_query, w_keyval=w_keyval, w_out=w_out, keys_cache=keys_cache, values_cache=values_cache, cached_len=cached_len)


rope_base = 500000.0
norm_eps = 1e-05

def rotate(values, positions):
    half = values.shape[-1] // 2
    index = jnp.arange(half).astype(jnp.float32)
    freqs = jnp.exp(-jnp.log(rope_base) * 2.0 * index / values.shape[-1])
    angles = positions.astype(jnp.float32)[:, None] * freqs[None, :]
    cos_table = jnp.cos(angles)[:, None, :]
    sin_table = jnp.sin(angles)[:, None, :]
    first_half = values[..., :half]
    second_half = values[..., half:]
    return jnp.concatenate([first_half * cos_table - second_half * sin_table, second_half * cos_table + first_half * sin_table], -1)

def layer_block(stream, gains, wq_layer, wkv_layer, wo_layer, cached_keys, cached_values, length):
    widened = stream.astype(jnp.float32)
    inverse_rms = lax.rsqrt(lax.optimization_barrier(jnp.mean(widened * widened, axis=-1, keepdims=True)) + norm_eps)
    normed = (widened * inverse_rms * gains.astype(jnp.float32)).astype(jnp.bfloat16)
    row_count = normed.shape[0]
    queries = jnp.dot(normed, wq_layer, preferred_element_type=jnp.float32)
    keyval = jnp.dot(normed, wkv_layer.reshape(wkv_layer.shape[0], -1), preferred_element_type=jnp.float32)
    kv_width = KVH * HD
    positions = length + jnp.arange(row_count).astype(jnp.int32)
    queries = rotate(queries.reshape(row_count, HQ, HD), positions).astype(jnp.bfloat16)
    new_keys = rotate(keyval[:, :kv_width].reshape(row_count, KVH, HD), positions).astype(jnp.bfloat16)
    new_values = keyval[:, kv_width:].reshape(row_count, KVH, HD).astype(jnp.bfloat16)
    slots = cached_keys.shape[0]
    all_keys = jnp.concatenate([cached_keys.reshape(slots, KVH, HD), new_keys], 0)
    all_values = jnp.concatenate([cached_values.reshape(slots, KVH, HD), new_values], 0)
    grouped = queries.reshape(row_count, KVH, HQ // KVH, HD)
    scores = jnp.einsum('tkgd,jkd->kgtj', grouped.astype(jnp.float32), all_keys.astype(jnp.float32)) * HD ** (-0.5)
    query_pos = jnp.arange(row_count)[:, None]
    key_pos = jnp.arange(slots + row_count)[None, :]
    visible = jnp.where(key_pos < slots, key_pos < length, key_pos - slots <= query_pos)
    scores = jnp.where(visible, scores, -1e+30)
    row_max = lax.optimization_barrier(jnp.max(scores, axis=-1, keepdims=True))
    exps = jnp.where(visible, jnp.exp(scores - row_max), 0.0)
    attn_probs = (exps / lax.optimization_barrier(jnp.sum(exps, axis=-1, keepdims=True))).astype(jnp.bfloat16)
    attended = jnp.einsum('kgtj,jkd->tkgd', attn_probs.astype(jnp.float32), all_values.astype(jnp.float32))
    attended = attended.astype(jnp.bfloat16).reshape(row_count, HQ * HD)
    group_cols = HQ * HD // N_TENSOR
    pieces = attended.reshape(row_count, N_TENSOR, group_cols).astype(jnp.float32)
    wo_groups = wo_layer.reshape(N_TENSOR, group_cols, wo_layer.shape[1]).astype(jnp.float32)
    partials = jnp.einsum('tjc,jcd->jtd', pieces, wo_groups).astype(jnp.bfloat16)
    partials = lax.optimization_barrier(partials).astype(jnp.float32)
    return lax.optimization_barrier(jnp.sum(partials, axis=0)).astype(jnp.bfloat16)

def reference(stream_two, block_last, incoming_two, incoming_last, norm_gain, w_query, w_keyval, w_out, keys_cache, values_cache, cached_len):
    current = stream_two
    carried = block_last
    streams = []
    blocks = []
    for tick_index in range(TICKS):
        lengths = cached_len[(LAYERS - 1 - jnp.arange(LAYERS) + tick_index).astype(jnp.int32)]

        def apply_layer(operands):
            return layer_block(*operands)
        produced = lax.map(apply_layer, (current, norm_gain, w_query, w_keyval, w_out, keys_cache[:, tick_index], values_cache[:, tick_index], lengths))
        formed = (current.astype(jnp.float32) + carried.astype(jnp.float32)).astype(jnp.bfloat16)
        streams.append(formed)
        blocks.append(produced)
        if tick_index + 1 < TICKS:
            current = jnp.concatenate([incoming_two[tick_index][None], formed[:-1]], 0)
            carried = jnp.concatenate([incoming_last[tick_index][None], produced[:-1]], 0)
    return (jnp.stack(streams, 1), jnp.stack(blocks, 1))
```

```python
import functools

import jax
import jax.numpy as jnp
from jax import lax
from jax.experimental import pallas as pl
from jax.experimental.pallas import tpu as pltpu
from jax.sharding import PartitionSpec as P

HD = 128
rope_base = 500000.0
norm_eps = 1e-05
bf16 = jnp.bfloat16
f32 = jnp.float32
Y = 4


def move(value, sections, tensors, target):
    pairs = []
    for s in range(sections):
        for t in range(tensors):
            s2, t2 = target(s, t)
            pairs.append((s * tensors + t, (s2 % sections) * tensors + t2))
    return lax.ppermute(value, ("section", "tensor"), pairs)


def y_shift(k):
    return lambda s, t: (s, (t & ~3) | ((t + k) & 3))


def hop(n, other=False):
    return lambda s, t: (s + n, t ^ 4 if other else t)


def rope_tables(length, rows):
    half = HD // 2
    index = jnp.arange(half).astype(f32)
    freqs = jnp.exp(-jnp.log(rope_base) * 2.0 * index / HD)
    positions = length + jnp.arange(rows)
    angles = positions.astype(f32)[:, None] * freqs[None, :]
    c, s = jnp.cos(angles), jnp.sin(angles)
    return jnp.concatenate([c, c], 1), jnp.concatenate([-s, s], 1)


def attend_kernel(
    scalars, g0, g1, g2, g3, gain, wq, wkv, wo, kc, vc, cos, sin, o0, o1, o2, o3, normed, att
):
    length, high, low = scalars[0], scalars[1], scalars[2]
    rows, width = g0.shape[1], g0.shape[2]
    pieces = (g0, g1, g2, g3)

    def chunk(slot, y):
        return ((high ^ slot) * Y + (y & (Y - 1))) * width

    total = jnp.zeros((rows, width), f32)
    for ref in pieces:
        for slot in range(2):
            v = ref[slot].astype(f32)
            total = total + v * v
    mean = jnp.sum(total, axis=-1, keepdims=True) / (2 * Y * width)
    inverse = lax.rsqrt(mean + norm_eps)
    for k, ref in enumerate(pieces):
        for slot in range(2):
            at = pl.ds(pl.multiple_of(chunk(slot, low - k + Y), width), width)
            scaled = ref[slot].astype(f32) * inverse * gain[:, at].astype(f32)
            normed[:, at] = scaled.astype(bf16)
    n = normed[...]
    q = jnp.dot(n, wq[...], preferred_element_type=f32)
    kv = jnp.dot(n, wkv[...], preferred_element_type=f32)
    cos_t, sin_t = cos[...], sin[...]

    def rotate(v):
        return (v * cos_t + pltpu.roll(v, HD // 2, 1) * sin_t).astype(bf16)

    heads = q.shape[1] // HD
    qs = jnp.concatenate([rotate(q[:, h * HD : (h + 1) * HD]) for h in range(heads)], 0)
    nk = rotate(kv[:, :HD])
    nv = kv[:, HD:].astype(bf16)
    contract = (((1,), (1,)), ((), ()))
    scale = HD ** (-0.5)
    s1 = lax.dot_general(qs, kc[...], contract, preferred_element_type=f32) * scale
    s2 = lax.dot_general(qs, nk, contract, preferred_element_type=f32) * scale
    seen1 = lax.broadcasted_iota(jnp.int32, s1.shape, 1) < length
    row = lax.broadcasted_iota(jnp.int32, s2.shape, 0) & (rows - 1)
    seen2 = lax.broadcasted_iota(jnp.int32, s2.shape, 1) <= row
    s1 = jnp.where(seen1, s1, -1e30)
    s2 = jnp.where(seen2, s2, -1e30)
    top = jnp.maximum(
        jnp.max(s1, axis=-1, keepdims=True), jnp.max(s2, axis=-1, keepdims=True)
    )
    e1 = jnp.where(seen1, jnp.exp(s1 - top), 0.0)
    e2 = jnp.where(seen2, jnp.exp(s2 - top), 0.0)
    norm = jnp.sum(e1, axis=-1, keepdims=True) + jnp.sum(e2, axis=-1, keepdims=True)
    p1 = (e1 / norm).astype(bf16)
    p2 = (e2 / norm).astype(bf16)
    out = jnp.dot(p1, vc[...], preferred_element_type=f32) + jnp.dot(
        p2, nv, preferred_element_type=f32
    )
    out = out.astype(bf16)
    for h in range(heads):
        att[:, h * HD : (h + 1) * HD] = out[h * rows : (h + 1) * rows]
    a = att[...]
    for k, ref in enumerate((o0, o1, o2, o3)):
        for slot in (1, 0):
            at = pl.ds(pl.multiple_of(chunk(slot, low + k), width), width)
            ref[slot] = jnp.dot(a, wo[:, at], preferred_element_type=f32).astype(bf16)


def attend(scalars, gathered, gain, wq, wkv, wo, kc, vc, cos, sin):
    _, rows, width = gathered[0].shape
    vmem = pl.BlockSpec(memory_space=pltpu.VMEM)
    cols = wq.shape[0]
    flops = 2 * rows * cols * (2 * wq.shape[1] + wkv.shape[1])
    return pl.pallas_call(
        attend_kernel,
        out_shape=[jax.ShapeDtypeStruct((2, rows, width), bf16)] * Y,
        in_specs=[pl.BlockSpec(memory_space=pltpu.SMEM)] + [vmem] * 12,
        out_specs=[vmem] * Y,
        scratch_shapes=[
            pltpu.VMEM((rows, cols), bf16),
            pltpu.VMEM((rows, wq.shape[1]), bf16),
        ],
        compiler_params=pltpu.CompilerParams(vmem_limit_bytes=40 * 1024 * 1024),
        cost_estimate=pl.CostEstimate(
            flops=flops, bytes_accessed=24 * 1024 * 1024, transcendentals=512 * 640
        ),
    )(scalars, *gathered, gain, wq, wkv, wo, kc, vc, cos, sin)


def body(
    stream_two, block_last, incoming_two, incoming_last, norm_gain,
    w_query, w_keyval, w_out, keys_cache, values_cache, cached_len,
):
    sections = lax.axis_size("section")
    tensors = lax.axis_size("tensor")
    sid = lax.axis_index("section")
    tid = lax.axis_index("tensor")
    rows = stream_two.shape[1]
    send = functools.partial(lambda v, f: move(v, sections, tensors, f))
    last = sections - 1

    def gather(pair):
        return [pair] + [send(pair, y_shift(k)) for k in range(1, Y)]

    def scatter(parts):
        got = [parts[0]] + [send(parts[k], y_shift(k)) for k in range(1, Y)]
        mine = sum(g[0].astype(f32) for g in got)
        theirs = sum(g[1].astype(f32) for g in got).astype(bf16)
        return (mine + send(theirs, hop(0, True)).astype(f32)).astype(bf16)

    def add(a, b):
        return (a.astype(f32) + b.astype(f32)).astype(bf16)

    wq, wo = w_query[0], w_out[0]
    wkv = w_keyval[0].reshape(w_keyval.shape[1], -1)

    def block(tick, gathered):
        length = cached_len[last - sid + tick]
        scalars = jnp.stack([length, tid // Y, tid % Y]).astype(jnp.int32)
        cos, sin = rope_tables(length, rows)
        return attend(
            scalars, gathered, norm_gain, wq, wkv, wo,
            keys_cache[0, tick], values_cache[0, tick], cos, sin,
        )

    x0 = stream_two[0]
    s0 = add(x0, block_last[0])
    pair0 = jnp.stack([x0, send(x0, hop(0, True))])
    parts0 = block(0, gather(pair0))

    out1 = jnp.where(sid == last, incoming_two[0], s0)
    a1 = send(out1, hop(1))
    pair1 = jnp.stack([a1, send(out1, hop(1, True))])
    parts1 = block(1, gather(pair1))
    base = send(pair1, hop(1))
    base = jnp.where(sid == 0, jnp.zeros_like(base), base)

    b0 = scatter(parts0)
    out2 = jnp.where(
        sid == last - 1, incoming_two[1], jnp.where(sid == last, incoming_last[0], b0)
    )
    pair2 = add(base, jnp.stack([send(out2, hop(2)), send(out2, hop(2, True))]))
    parts2 = block(2, gather(pair2))

    b1 = scatter(parts1)
    t1 = add(a1, send(jnp.where(sid == last, incoming_last[0], b0), hop(1)))
    t2 = add(pair2[0], send(jnp.where(sid == last, incoming_last[1], b1), hop(1)))
    b2 = scatter(parts2)
    return jnp.stack([s0, t1, t2])[None], jnp.stack([b0, b1, b2])[None]


def solution(mesh):
    placed = (
        P("section", None, "tensor"),
        P("section", None, "tensor"),
        P(None, None, "tensor"),
        P(None, None, "tensor"),
        P("section", None),
        P("section", None, "tensor"),
        P("section", None, None, "tensor"),
        P("section", "tensor", None),
        P("section", None, None, "tensor"),
        P("section", None, None, "tensor"),
        P(),
    )
    out = P("section", None, None, "tensor")
    return jax.shard_map(
        body, mesh=mesh, in_specs=placed, out_specs=(out, out), check_vma=False
    )
```

```python
import functools

import jax
import jax.numpy as jnp
from jax import lax
from jax.experimental import pallas as pl
from jax.experimental.pallas import tpu as pltpu
from jax.sharding import PartitionSpec as P

HD = 128
rope_base = 500000.0
norm_eps = 1e-05
bf16 = jnp.bfloat16
f32 = jnp.float32
Y = 4
ORDER = (3, 1, 2)


def move(value, sections, tensors, target):
    pairs = []
    for s in range(sections):
        for t in range(tensors):
            s2, t2 = target(s, t)
            if s2 >= sections:
                s2, t2 = s2 - sections, t ^ 4
            pairs.append((s * tensors + t, s2 * tensors + t2))
    return lax.ppermute(value, ("section", "tensor"), pairs)


def y_shift(k):
    return lambda s, t: (s, (t & ~3) | ((t + k) & 3))


def hop(n, other=False):
    return lambda s, t: (s + n, t ^ 4 if other else t)


def rope_tables(lengths, rows):
    half = HD // 2
    index = jnp.arange(half).astype(f32)
    freqs = jnp.exp(-jnp.log(rope_base) * 2.0 * index / HD)
    positions = lengths[:, None] + jnp.arange(rows)
    angles = positions.astype(f32)[..., None] * freqs
    return jnp.cos(angles), jnp.sin(angles)


def attend_kernel(tick, *refs):
    scalars, pieces, refs = refs[0], refs[1 : 1 + Y], refs[1 + Y :]
    gain, cos, sin, wq_hbm, wkv_hbm, wo_hbm, kc_hbm, vc_hbm = refs[:8]
    outs, refs = refs[8 : 8 + Y], refs[8 + Y :]
    wq, wkv, wo, kc, vc, att, sems = refs
    length, high, low = scalars[tick], scalars[3], scalars[4]

    taken = {k: [ref.at[0], ref.at[1]] for k, ref in zip((0,) + ORDER, pieces)}
    given = [[ref.at[0], ref.at[1]] for ref in outs]
    rows, width = taken[0][0].shape

    def chunk(slot, y):
        at = ((high ^ slot) * Y + (y & (Y - 1))) * width
        return pl.ds(pl.multiple_of(at, width), width)

    order = [(k, slot) for k in range(Y) for slot in range(2)]
    spots = [chunk(slot, low - k + Y) for k, slot in order]
    loads = []
    for i, at in enumerate(spots):
        loads.append(
            (
                pltpu.make_async_copy(wq_hbm.at[at], wq.at[at], sems.at[2 * i]),
                pltpu.make_async_copy(wkv_hbm.at[at], wkv.at[at], sems.at[2 * i + 1]),
            )
        )
    n = 2 * len(order)
    load_k = pltpu.make_async_copy(kc_hbm.at[0, tick], kc, sems.at[n])
    load_v = pltpu.make_async_copy(vc_hbm.at[0, tick], vc, sems.at[n + 1])
    load_o = pltpu.make_async_copy(wo_hbm, wo, sems.at[n + 2])
    for a, b in loads:
        a.start()
        b.start()
    load_k.start()
    load_v.start()
    load_o.start()

    total = jnp.zeros((rows, width), f32)
    for k, slot in order:
        v = taken[k][slot][...].astype(f32)
        total = total + v * v
    mean = jnp.sum(total, axis=-1, keepdims=True) / (2 * Y * width)
    inverse = lax.rsqrt(mean + norm_eps)
    q = jnp.zeros((rows, wq.shape[1]), f32)
    kv = jnp.zeros((rows, wkv.shape[1]), f32)
    for i, (k, slot) in enumerate(order):
        at = spots[i]
        v = taken[k][slot][...].astype(f32)
        normed = (v * inverse * gain[:, at].astype(f32)).astype(bf16)
        loads[i][0].wait()
        loads[i][1].wait()
        q = q + jnp.dot(normed, wq[at, :], preferred_element_type=f32)
        kv = kv + jnp.dot(normed, wkv[at, :], preferred_element_type=f32)
    c, s = cos[tick], sin[tick]
    cos_t, sin_t = jnp.concatenate([c, c], 1), jnp.concatenate([-s, s], 1)

    def rotate(v):
        return (v * cos_t + pltpu.roll(v, HD // 2, 1) * sin_t).astype(bf16)

    heads = q.shape[1] // HD
    qs = jnp.concatenate([rotate(q[:, h * HD : (h + 1) * HD]) for h in range(heads)], 0)
    nk = rotate(kv[:, :HD])
    nv = kv[:, HD:].astype(bf16)
    contract = (((1,), (1,)), ((), ()))
    scale = HD ** (-0.5)
    load_k.wait()
    s1 = lax.dot_general(qs, kc[...], contract, preferred_element_type=f32) * scale
    s2 = lax.dot_general(qs, nk, contract, preferred_element_type=f32) * scale
    seen1 = lax.broadcasted_iota(jnp.int32, s1.shape, 1) < length
    row = lax.broadcasted_iota(jnp.int32, s2.shape, 0) & (rows - 1)
    seen2 = lax.broadcasted_iota(jnp.int32, s2.shape, 1) <= row
    s1 = jnp.where(seen1, s1, -1e30)
    s2 = jnp.where(seen2, s2, -1e30)
    top = jnp.maximum(
        jnp.max(s1, axis=-1, keepdims=True), jnp.max(s2, axis=-1, keepdims=True)
    )
    e1 = jnp.where(seen1, jnp.exp(s1 - top), 0.0)
    e2 = jnp.where(seen2, jnp.exp(s2 - top), 0.0)
    norm = jnp.sum(e1, axis=-1, keepdims=True) + jnp.sum(e2, axis=-1, keepdims=True)
    p1 = (e1 / norm).astype(bf16)
    p2 = (e2 / norm).astype(bf16)
    load_v.wait()
    out = jnp.dot(p1, vc[...], preferred_element_type=f32) + jnp.dot(
        p2, nv, preferred_element_type=f32
    )
    out = out.astype(bf16)
    for h in range(heads):
        att[:, h * HD : (h + 1) * HD] = out[h * rows : (h + 1) * rows]
    a = att[...]
    load_o.wait()
    for slot in (1, 0):
        for k in range(Y):
            at = chunk(slot, low + k)
            given[k][slot][...] = jnp.dot(a, wo[:, at], preferred_element_type=f32).astype(bf16)


def attend(tick, scalars, gathered, gain, cos, sin, wq, wkv, wo, kc, vc):
    rows, width = gathered[0].shape[-2:]
    vmem, hbm = pl.BlockSpec(memory_space=pltpu.VMEM), pl.BlockSpec(memory_space=pltpu.HBM)
    cols = wq.shape[0]
    out_shape = [jax.ShapeDtypeStruct((2, rows, width), bf16)] * Y
    flops = 2 * rows * cols * (2 * wq.shape[1] + wkv.shape[1])
    return pl.pallas_call(
        functools.partial(attend_kernel, tick),
        out_shape=out_shape,
        in_specs=[pl.BlockSpec(memory_space=pltpu.SMEM)]
        + [vmem] * (len(gathered) + 3)
        + [hbm] * 5,
        out_specs=[vmem] * len(out_shape),
        scratch_shapes=[
            pltpu.VMEM(wq.shape, bf16),
            pltpu.VMEM(wkv.shape, bf16),
            pltpu.VMEM(wo.shape, bf16),
            pltpu.VMEM(kc.shape[2:], bf16),
            pltpu.VMEM(vc.shape[2:], bf16),
            pltpu.VMEM((rows, wq.shape[1]), bf16),
            pltpu.SemaphoreType.DMA((4 * Y + 3,)),
        ],
        compiler_params=pltpu.CompilerParams(vmem_limit_bytes=22 * 1024 * 1024),
        cost_estimate=pl.CostEstimate(
            flops=flops, bytes_accessed=40 * 1024 * 1024, transcendentals=512 * 640
        ),
    )(scalars, *gathered, gain, cos, sin, wq, wkv, wo, kc, vc)


def combine_kernel(where, own, other, base, local, out):
    first, entry = where[0] == 0, where[0] < 2
    for slot in range(2):
        moved = own[slot].astype(f32) + other[1 - slot].astype(f32)
        fresh = local[...] if slot == 0 else own[0]
        moved = jnp.where(entry, fresh, moved.astype(bf16)).astype(f32)
        out[slot] = jnp.where(first, moved, base[slot].astype(f32) + moved).astype(bf16)


def combine(where, own, other, base, local):
    vmem = pl.BlockSpec(memory_space=pltpu.VMEM)
    return pl.pallas_call(
        combine_kernel,
        out_shape=jax.ShapeDtypeStruct(own.shape, own.dtype),
        in_specs=[pl.BlockSpec(memory_space=pltpu.SMEM)] + [vmem] * 4,
        out_specs=vmem,
        compiler_params=pltpu.CompilerParams(vmem_limit_bytes=4 * 1024 * 1024),
    )(where, own, other, base, local)


def body(
    stream_two, block_last, incoming_two, incoming_last, norm_gain,
    w_query, w_keyval, w_out, keys_cache, values_cache, cached_len,
):
    sections = lax.axis_size("section")
    tensors = lax.axis_size("tensor")
    sid = lax.axis_index("section")
    tid = lax.axis_index("tensor")
    rows = stream_two.shape[1]
    send = functools.partial(lambda v, f: move(v, sections, tensors, f))
    last = sections - 1
    first, final = sid == 0, sid == last

    def after(value, *others):
        return lax.optimization_barrier((value, others))[0]

    def exchange(parts):
        return [parts[0]] + [send(parts[k], y_shift(k)) for k in ORDER]

    def gather(pair):
        return exchange([pair] * Y)

    def add(a, b):
        return (a.astype(f32) + b.astype(f32)).astype(bf16)

    def halves(got):
        both = sum(g.astype(f32) for g in got)
        return both[0], both[1].astype(bf16)

    x0 = stream_two[0]
    pair0 = jnp.stack([x0, send(x0, hop(0, True))])
    wq = pltpu.with_memory_space_constraint(w_query[0], pltpu.HBM)
    wo = pltpu.with_memory_space_constraint(w_out[0], pltpu.HBM)

    ticks = keys_cache.shape[1]
    lengths = lax.dynamic_slice_in_dim(cached_len, last - sid, ticks)
    scalars = jnp.concatenate([lengths, jnp.stack([tid // Y, tid % Y]).astype(jnp.int32)])
    cos, sin = rope_tables(lengths, rows)
    wkv = w_keyval[0].reshape(w_keyval.shape[1], -1)

    pair0, scalars, cos, sin, wkv = lax.optimization_barrier(
        (pair0, scalars, cos, sin, wkv)
    )
    all0 = gather(pair0)
    wkv = pltpu.with_memory_space_constraint(wkv, pltpu.HBM)

    def block(tick, gathered):
        return attend(
            tick, scalars, gathered, norm_gain, cos, sin,
            wq, wkv, wo, keys_cache, values_cache,
        )

    parts0 = block(0, all0)
    got0 = exchange(parts0)
    block_late, enter_two, enter_last = after(
        (block_last, incoming_two, incoming_last), parts0
    )
    out1 = jnp.where(final, enter_two[0], add(x0, block_late[0]))
    a1, z1 = send(out1, hop(1)), send(out1, hop(1, True))
    local = jnp.where(first, enter_two[1], enter_last[0])
    entering = jnp.where(final, enter_last[0], enter_two[1])
    got0, local, entering = lax.optimization_barrier((got0, local, entering))
    sums0 = sum(g.astype(f32) for g in got0).astype(bf16)
    out2 = jnp.where(sid >= last - 1, entering[None], sums0)
    own, other = send(out2, hop(2)), send(out2, hop(2, True))
    a1, z1 = after((a1, z1), out2)
    a1 = jnp.where(first, incoming_two[0], a1)
    pair1 = jnp.stack([a1, z1])
    base = send(pair1, hop(1))
    all1 = gather(pair1)
    pair2 = combine(sid.astype(jnp.int32)[None], own, other, base, local)
    all2 = gather(pair2)
    late0, all1 = after((sums0, all1), pair2)
    swapped0 = send(late0[1], hop(0, True))
    parts1 = block(1, all1)
    got1 = exchange(parts1)
    parts2 = block(2, after(all2, parts1))
    swapped0, got1 = after((swapped0, got1), parts2)
    got2 = lax.optimization_barrier(exchange(parts2))

    mine1, theirs1 = halves(got1)
    b1 = (mine1 + send(theirs1, hop(0, True)).astype(f32)).astype(bf16)
    b0 = add(late0[0], swapped0)
    s0 = add(x0, block_last[0])
    t1 = add(a1, jnp.where(first, incoming_last[0], send(b0, hop(1))))
    t2 = add(pair2[0], jnp.where(first, incoming_last[1], send(b1, hop(1))))
    mine2, theirs2 = halves(got2)
    b2 = (mine2 + send(theirs2, hop(0, True)).astype(f32)).astype(bf16)
    return jnp.stack([s0, t1, t2])[None], jnp.stack([b0, b1, b2])[None]


def solution(mesh):
    placed = (
        P("section", None, "tensor"),
        P("section", None, "tensor"),
        P(None, None, "tensor"),
        P(None, None, "tensor"),
        P("section", None),
        P("section", None, "tensor"),
        P("section", None, None, "tensor"),
        P("section", "tensor", None),
        P("section", None, None, "tensor"),
        P("section", None, None, "tensor"),
        P(),
    )
    out = P("section", None, None, "tensor")
    return jax.shard_map(
        body, mesh=mesh, in_specs=placed, out_specs=(out, out), check_vma=False
    )
```

```python
import functools

import jax
import jax.numpy as jnp
from jax import lax
from jax.experimental import pallas as pl
from jax.experimental.pallas import tpu as pltpu
from jax.sharding import PartitionSpec as P

HD = 128
rope_base = 500000.0
norm_eps = 1e-05
bf16 = jnp.bfloat16
f32 = jnp.float32
Y = 4
ORDER = (3, 1, 2)


def move(value, sections, tensors, target):
    pairs = []
    for s in range(sections):
        for t in range(tensors):
            s2, t2 = target(s, t)
            if s2 >= sections:
                s2, t2 = s2 - sections, t ^ 4
            pairs.append((s * tensors + t, s2 * tensors + t2))
    return lax.ppermute(value, ("section", "tensor"), pairs)


def y_shift(k):
    return lambda s, t: (s, (t & ~3) | ((t + k) & 3))


def hop(n, other=False):
    return lambda s, t: (s + n, t ^ 4 if other else t)


def rope_tables(lengths, rows):
    half = HD // 2
    index = jnp.arange(half).astype(f32)
    freqs = jnp.exp(-jnp.log(rope_base) * 2.0 * index / HD)
    positions = lengths[:, None] + jnp.arange(rows)
    angles = positions.astype(f32)[..., None] * freqs
    return jnp.cos(angles), jnp.sin(angles)


def attend_kernel(tick, *refs):
    scalars, pieces, refs = refs[0], refs[1 : 1 + Y], refs[1 + Y :]
    gain, cos, sin, wq_hbm, wkv_hbm, wo_hbm, kc_hbm, vc_hbm = refs[:8]
    outs, refs = refs[8 : 8 + Y], refs[8 + Y :]
    wq, wkv, wo, kc, vc, att, sems = refs
    length, high, low = scalars[tick], scalars[3], scalars[4]

    taken = {k: [ref.at[0], ref.at[1]] for k, ref in zip((0,) + ORDER, pieces)}
    given = [[ref.at[0], ref.at[1]] for ref in outs]
    rows, width = taken[0][0].shape

    def chunk(slot, y):
        at = ((high ^ slot) * Y + (y & (Y - 1))) * width
        return pl.ds(pl.multiple_of(at, width), width)

    order = [(k, slot) for k in range(Y) for slot in range(2)]
    spots = [chunk(slot, low - k + Y) for k, slot in order]
    loads = []
    for i, at in enumerate(spots):
        loads.append(
            (
                pltpu.make_async_copy(wq_hbm.at[at], wq.at[at], sems.at[2 * i]),
                pltpu.make_async_copy(wkv_hbm.at[at], wkv.at[at], sems.at[2 * i + 1]),
            )
        )
    n = 2 * len(order)
    load_k = pltpu.make_async_copy(kc_hbm.at[0, tick], kc, sems.at[n])
    load_v = pltpu.make_async_copy(vc_hbm.at[0, tick], vc, sems.at[n + 1])
    load_o = pltpu.make_async_copy(wo_hbm, wo, sems.at[n + 2])
    for a, b in loads:
        a.start()
        b.start()
    load_k.start()
    load_v.start()
    load_o.start()

    total = jnp.zeros((rows, width), f32)
    for k, slot in order:
        v = taken[k][slot][...].astype(f32)
        total = total + v * v
    mean = jnp.sum(total, axis=-1, keepdims=True) / (2 * Y * width)
    inverse = lax.rsqrt(mean + norm_eps)
    q = jnp.zeros((rows, wq.shape[1]), f32)
    kv = jnp.zeros((rows, wkv.shape[1]), f32)
    for i, (k, slot) in enumerate(order):
        at = spots[i]
        v = taken[k][slot][...].astype(f32)
        normed = (v * inverse * gain[:, at].astype(f32)).astype(bf16)
        loads[i][0].wait()
        loads[i][1].wait()
        q = q + jnp.dot(normed, wq[at, :], preferred_element_type=f32)
        kv = kv + jnp.dot(normed, wkv[at, :], preferred_element_type=f32)
    c, s = cos[tick], sin[tick]
    cos_t, sin_t = jnp.concatenate([c, c], 1), jnp.concatenate([-s, s], 1)

    def rotate(v):
        return (v * cos_t + pltpu.roll(v, HD // 2, 1) * sin_t).astype(bf16)

    heads = q.shape[1] // HD
    qs = jnp.concatenate([rotate(q[:, h * HD : (h + 1) * HD]) for h in range(heads)], 0)
    nk = rotate(kv[:, :HD])
    nv = kv[:, HD:].astype(bf16)
    contract = (((1,), (1,)), ((), ()))
    scale = HD ** (-0.5)
    load_k.wait()
    s1 = lax.dot_general(qs, kc[...], contract, preferred_element_type=f32) * scale
    s2 = lax.dot_general(qs, nk, contract, preferred_element_type=f32) * scale
    seen1 = lax.broadcasted_iota(jnp.int32, s1.shape, 1) < length
    row = lax.broadcasted_iota(jnp.int32, s2.shape, 0) & (rows - 1)
    seen2 = lax.broadcasted_iota(jnp.int32, s2.shape, 1) <= row
    s1 = jnp.where(seen1, s1, -1e30)
    s2 = jnp.where(seen2, s2, -1e30)
    top = jnp.maximum(
        jnp.max(s1, axis=-1, keepdims=True), jnp.max(s2, axis=-1, keepdims=True)
    )
    e1 = jnp.where(seen1, jnp.exp(s1 - top), 0.0)
    e2 = jnp.where(seen2, jnp.exp(s2 - top), 0.0)
    norm = jnp.sum(e1, axis=-1, keepdims=True) + jnp.sum(e2, axis=-1, keepdims=True)
    p1 = (e1 / norm).astype(bf16)
    p2 = (e2 / norm).astype(bf16)
    load_v.wait()
    out = jnp.dot(p1, vc[...], preferred_element_type=f32) + jnp.dot(
        p2, nv, preferred_element_type=f32
    )
    out = out.astype(bf16)
    for h in range(heads):
        att[:, h * HD : (h + 1) * HD] = out[h * rows : (h + 1) * rows]
    a = att[...]
    load_o.wait()
    for slot in (1, 0):
        for k in range(Y):
            at = chunk(slot, low + k)
            given[k][slot][...] = jnp.dot(a, wo[:, at], preferred_element_type=f32).astype(bf16)


def attend(tick, scalars, gathered, gain, cos, sin, wq, wkv, wo, kc, vc):
    rows, width = gathered[0].shape[-2:]
    vmem, hbm = pl.BlockSpec(memory_space=pltpu.VMEM), pl.BlockSpec(memory_space=pltpu.HBM)
    cols = wq.shape[0]
    out_shape = [jax.ShapeDtypeStruct((2, rows, width), bf16)] * Y
    flops = 2 * rows * cols * (2 * wq.shape[1] + wkv.shape[1])
    return pl.pallas_call(
        functools.partial(attend_kernel, tick),
        out_shape=out_shape,
        in_specs=[pl.BlockSpec(memory_space=pltpu.SMEM)]
        + [vmem] * (len(gathered) + 3)
        + [hbm] * 5,
        out_specs=[vmem] * len(out_shape),
        scratch_shapes=[
            pltpu.VMEM(wq.shape, bf16),
            pltpu.VMEM(wkv.shape, bf16),
            pltpu.VMEM(wo.shape, bf16),
            pltpu.VMEM(kc.shape[2:], bf16),
            pltpu.VMEM(vc.shape[2:], bf16),
            pltpu.VMEM((rows, wq.shape[1]), bf16),
            pltpu.SemaphoreType.DMA((4 * Y + 3,)),
        ],
        compiler_params=pltpu.CompilerParams(vmem_limit_bytes=22 * 1024 * 1024),
        cost_estimate=pl.CostEstimate(
            flops=flops, bytes_accessed=40 * 1024 * 1024, transcendentals=512 * 640
        ),
    )(scalars, *gathered, gain, cos, sin, wq, wkv, wo, kc, vc)


def combine_kernel(where, own, other, base, local, out):
    first, entry = where[0] == 0, where[0] < 2
    for slot in range(2):
        moved = own[slot].astype(f32) + other[1 - slot].astype(f32)
        fresh = local[...] if slot == 0 else own[0]
        moved = jnp.where(entry, fresh, moved.astype(bf16)).astype(f32)
        out[slot] = jnp.where(first, moved, base[slot].astype(f32) + moved).astype(bf16)


def combine(where, own, other, base, local):
    vmem = pl.BlockSpec(memory_space=pltpu.VMEM)
    return pl.pallas_call(
        combine_kernel,
        out_shape=jax.ShapeDtypeStruct(own.shape, own.dtype),
        in_specs=[pl.BlockSpec(memory_space=pltpu.SMEM)] + [vmem] * 4,
        out_specs=vmem,
        compiler_params=pltpu.CompilerParams(vmem_limit_bytes=4 * 1024 * 1024),
    )(where, own, other, base, local)


def body(
    stream_two, block_last, incoming_two, incoming_last, norm_gain,
    w_query, w_keyval, w_out, keys_cache, values_cache, cached_len,
):
    sections = lax.axis_size("section")
    tensors = lax.axis_size("tensor")
    sid = lax.axis_index("section")
    tid = lax.axis_index("tensor")
    rows = stream_two.shape[1]
    send = functools.partial(lambda v, f: move(v, sections, tensors, f))
    last = sections - 1
    first, final = sid == 0, sid == last

    def after(value, *others):
        return lax.optimization_barrier((value, others))[0]

    def exchange(parts):
        return [parts[0]] + [send(parts[k], y_shift(k)) for k in ORDER]

    def gather(pair):
        return exchange([pair] * Y)

    def add(a, b):
        return (a.astype(f32) + b.astype(f32)).astype(bf16)

    def halves(got):
        both = sum(g.astype(f32) for g in got)
        return both[0], both[1].astype(bf16)

    x0 = stream_two[0]
    pair0 = jnp.stack([x0, send(x0, hop(0, True))])
    wq = pltpu.with_memory_space_constraint(w_query[0], pltpu.HBM)
    wo = pltpu.with_memory_space_constraint(w_out[0], pltpu.HBM)

    ticks = keys_cache.shape[1]
    lengths = lax.dynamic_slice_in_dim(cached_len, last - sid, ticks)
    scalars = jnp.concatenate([lengths, jnp.stack([tid // Y, tid % Y]).astype(jnp.int32)])
    cos, sin = rope_tables(lengths, rows)
    wkv = w_keyval[0].reshape(w_keyval.shape[1], -1)

    pair0, scalars, cos, sin, wkv = lax.optimization_barrier(
        (pair0, scalars, cos, sin, wkv)
    )
    all0 = gather(pair0)
    wkv = pltpu.with_memory_space_constraint(wkv, pltpu.HBM)

    def block(tick, gathered):
        return attend(
            tick, scalars, gathered, norm_gain, cos, sin,
            wq, wkv, wo, keys_cache, values_cache,
        )

    early = after(block_last, all0[1])
    other1 = jnp.where(final, incoming_two[0], add(x0, early[0]))
    z1 = send(other1, hop(1, True))

    parts0 = block(0, all0)
    got0 = exchange(parts0)
    own1, enter_two, enter_last = after((other1, incoming_two, incoming_last), parts0)
    a1 = send(own1, hop(1))
    local = jnp.where(first, enter_two[1], enter_last[0])
    entering = jnp.where(final, enter_last[0], enter_two[1])
    got0, local, entering, a1 = lax.optimization_barrier((got0, local, entering, a1))
    sums0 = sum(g.astype(f32) for g in got0).astype(bf16)
    out2 = jnp.where(sid >= last - 1, entering[None], sums0)
    own, other = send(out2, hop(2)), send(out2, hop(2, True))
    a1, z1 = after((a1, z1), out2)
    a1 = jnp.where(first, incoming_two[0], a1)
    pair1 = jnp.stack([a1, z1])
    base = send(pair1, hop(1))
    all1 = gather(pair1)
    pair2 = combine(sid.astype(jnp.int32)[None], own, other, base, local)
    all2 = gather(pair2)
    parts1 = block(1, after(all1, pair2))
    got1 = exchange(parts1)
    parts2 = block(2, after(all2, parts1))
    sums0, got1 = after((sums0, got1), parts2)
    got2 = lax.optimization_barrier(exchange(parts2))
    mine2, theirs2 = halves(got2)

    swapped0 = send(sums0[1], hop(0, True))
    mine1, theirs1 = halves(got1)
    swapped1 = send(theirs1, hop(0, True))
    swapped0, swapped1 = after((swapped0, swapped1), theirs2)
    b0 = add(sums0[0], swapped0)
    b1 = (mine1 + swapped1.astype(f32)).astype(bf16)
    s0 = add(x0, block_last[0])
    back = send(jnp.stack([b0, b1]), hop(1))
    t1 = add(a1, jnp.where(first, incoming_last[0], back[0]))
    t2 = add(pair2[0], jnp.where(first, incoming_last[1], back[1]))
    b2 = (mine2 + send(theirs2, hop(0, True)).astype(f32)).astype(bf16)
    return jnp.stack([s0, t1, t2])[None], jnp.stack([b0, b1, b2])[None]


def solution(mesh):
    placed = (
        P("section", None, "tensor"),
        P("section", None, "tensor"),
        P(None, None, "tensor"),
        P(None, None, "tensor"),
        P("section", None),
        P("section", None, "tensor"),
        P("section", None, None, "tensor"),
        P("section", "tensor", None),
        P("section", None, None, "tensor"),
        P("section", None, None, "tensor"),
        P(),
    )
    out = P("section", None, None, "tensor")
    return jax.shard_map(
        body, mesh=mesh, in_specs=placed, out_specs=(out, out), check_vma=False
    )
```

```python
import functools

import jax
import jax.numpy as jnp
from jax import lax
from jax.experimental import pallas as pl
from jax.experimental.pallas import tpu as pltpu
from jax.sharding import PartitionSpec as P

HD = 128
rope_base = 500000.0
norm_eps = 1e-05
bf16 = jnp.bfloat16
f32 = jnp.float32
Y = 4
ORDER = (3, 1, 2)


def move(value, sections, tensors, target):
    pairs = []
    for s in range(sections):
        for t in range(tensors):
            s2, t2 = target(s, t)
            if s2 >= sections:
                s2, t2 = s2 - sections, t ^ 4
            pairs.append((s * tensors + t, s2 * tensors + t2))
    return lax.ppermute(value, ("section", "tensor"), pairs)


def y_shift(k):
    return lambda s, t: (s, (t & ~3) | ((t + k) & 3))


def hop(n, other=False):
    return lambda s, t: (s + n, t ^ 4 if other else t)


def rope_tables(lengths, rows):
    half = HD // 2
    index = jnp.arange(half).astype(f32)
    freqs = jnp.exp(-jnp.log(rope_base) * 2.0 * index / HD)
    positions = lengths[:, None] + jnp.arange(rows)
    angles = positions.astype(f32)[..., None] * freqs
    return jnp.cos(angles), jnp.sin(angles)


def attend_kernel(tick, held, *refs):
    scalars, pieces, refs = refs[0], refs[1 : 1 + Y], refs[1 + Y :]
    gain, cos, sin, wq_hbm, wkv_hbm, wo_hbm, kc_hbm, vc_hbm = refs[:8]
    outs, refs = refs[8 : 8 + Y], refs[8 + Y :]
    if held:
        wq, wkv, wo = wq_hbm, wkv_hbm, wo_hbm
    else:
        wq, wkv, wo = refs[:3]
    kc, vc, att, sems = refs[-4:]
    length, high, low = scalars[tick], scalars[3], scalars[4]

    taken = {k: [ref.at[0], ref.at[1]] for k, ref in zip((0,) + ORDER, pieces)}
    given = [[ref.at[0], ref.at[1]] for ref in outs]
    rows, width = taken[0][0].shape

    def chunk(slot, y):
        at = ((high ^ slot) * Y + (y & (Y - 1))) * width
        return pl.ds(pl.multiple_of(at, width), width)

    order = [(k, slot) for k in range(Y) for slot in range(2)]
    spots = [chunk(slot, low - k + Y) for k, slot in order]
    loads = []
    for i, at in enumerate(() if held else spots):
        loads.append(
            (
                pltpu.make_async_copy(wq_hbm.at[at], wq.at[at], sems.at[2 * i]),
                pltpu.make_async_copy(wkv_hbm.at[at], wkv.at[at], sems.at[2 * i + 1]),
            )
        )
    n = 2 * len(order)
    load_k = pltpu.make_async_copy(kc_hbm.at[0, tick], kc, sems.at[n])
    load_v = pltpu.make_async_copy(vc_hbm.at[0, tick], vc, sems.at[n + 1])
    if not held:
        load_o = pltpu.make_async_copy(wo_hbm, wo, sems.at[n + 2])
    if not held:
        for a, b in loads:
            a.start()
            b.start()
    load_k.start()
    load_v.start()
    if not held:
        load_o.start()

    total = jnp.zeros((rows, width), f32)
    for k, slot in order:
        v = taken[k][slot][...].astype(f32)
        total = total + v * v
    mean = jnp.sum(total, axis=-1, keepdims=True) / (2 * Y * width)
    inverse = lax.rsqrt(mean + norm_eps)
    q = jnp.zeros((rows, wq.shape[1]), f32)
    kv = jnp.zeros((rows, wkv.shape[1]), f32)
    for i, (k, slot) in enumerate(order):
        at = spots[i]
        v = taken[k][slot][...].astype(f32)
        normed = (v * inverse * gain[:, at].astype(f32)).astype(bf16)
        if not held:
            loads[i][0].wait()
            loads[i][1].wait()
        q = q + jnp.dot(normed, wq[at, :], preferred_element_type=f32)
        kv = kv + jnp.dot(normed, wkv[at, :], preferred_element_type=f32)
    c, s = cos[tick], sin[tick]
    cos_t, sin_t = jnp.concatenate([c, c], 1), jnp.concatenate([-s, s], 1)

    def rotate(v):
        return (v * cos_t + pltpu.roll(v, HD // 2, 1) * sin_t).astype(bf16)

    heads = q.shape[1] // HD
    qs = jnp.concatenate([rotate(q[:, h * HD : (h + 1) * HD]) for h in range(heads)], 0)
    nk = rotate(kv[:, :HD])
    nv = kv[:, HD:].astype(bf16)
    contract = (((1,), (1,)), ((), ()))
    scale = HD ** (-0.5)
    load_k.wait()
    s1 = lax.dot_general(qs, kc[...], contract, preferred_element_type=f32) * scale
    s2 = lax.dot_general(qs, nk, contract, preferred_element_type=f32) * scale
    seen1 = lax.broadcasted_iota(jnp.int32, s1.shape, 1) < length
    row = lax.broadcasted_iota(jnp.int32, s2.shape, 0) & (rows - 1)
    seen2 = lax.broadcasted_iota(jnp.int32, s2.shape, 1) <= row
    s1 = jnp.where(seen1, s1, -1e30)
    s2 = jnp.where(seen2, s2, -1e30)
    top = jnp.maximum(
        jnp.max(s1, axis=-1, keepdims=True), jnp.max(s2, axis=-1, keepdims=True)
    )
    e1 = jnp.where(seen1, jnp.exp(s1 - top), 0.0)
    e2 = jnp.where(seen2, jnp.exp(s2 - top), 0.0)
    norm = jnp.sum(e1, axis=-1, keepdims=True) + jnp.sum(e2, axis=-1, keepdims=True)
    p1 = (e1 / norm).astype(bf16)
    p2 = (e2 / norm).astype(bf16)
    load_v.wait()
    out = jnp.dot(p1, vc[...], preferred_element_type=f32) + jnp.dot(
        p2, nv, preferred_element_type=f32
    )
    out = out.astype(bf16)
    for h in range(heads):
        att[:, h * HD : (h + 1) * HD] = out[h * rows : (h + 1) * rows]
    a = att[...]
    if not held:
        load_o.wait()
    for slot in (1, 0):
        for k in range(Y):
            at = chunk(slot, low + k)
            given[k][slot][...] = jnp.dot(a, wo[:, at], preferred_element_type=f32).astype(bf16)


def attend(tick, held, scalars, gathered, gain, cos, sin, wq, wkv, wo, kc, vc):
    rows, width = gathered[0].shape[-2:]
    vmem, hbm = pl.BlockSpec(memory_space=pltpu.VMEM), pl.BlockSpec(memory_space=pltpu.HBM)
    cols = wq.shape[0]
    out_shape = [jax.ShapeDtypeStruct((2, rows, width), bf16)] * Y
    flops = 2 * rows * cols * (2 * wq.shape[1] + wkv.shape[1])
    return pl.pallas_call(
        functools.partial(attend_kernel, tick, held),
        out_shape=out_shape,
        in_specs=[pl.BlockSpec(memory_space=pltpu.SMEM)]
        + [vmem] * (len(gathered) + 3)
        + [vmem if held else hbm] * 3
        + [hbm] * 2,
        out_specs=[vmem] * len(out_shape),
        scratch_shapes=([] if held else [pltpu.VMEM(w.shape, bf16) for w in (wq, wkv, wo)])
        + [
            pltpu.VMEM(kc.shape[2:], bf16),
            pltpu.VMEM(vc.shape[2:], bf16),
            pltpu.VMEM((rows, wq.shape[1]), bf16),
            pltpu.SemaphoreType.DMA((4 * Y + 3,)),
        ],
        compiler_params=pltpu.CompilerParams(vmem_limit_bytes=22 * 1024 * 1024),
        cost_estimate=pl.CostEstimate(
            flops=flops, bytes_accessed=40 * 1024 * 1024, transcendentals=512 * 640
        ),
    )(scalars, *gathered, gain, cos, sin, wq, wkv, wo, kc, vc)


def load_kernel(wq, wkv, wo, wq_out, wkv_out, wo_out, sems):
    copies = [
        pltpu.make_async_copy(a, b, sems.at[i])
        for i, (a, b) in enumerate(((wq, wq_out), (wkv, wkv_out), (wo, wo_out)))
    ]
    for copy in copies:
        copy.start()
    for copy in copies:
        copy.wait()


def load(wq, wkv, wo):
    hbm, vmem = pl.BlockSpec(memory_space=pltpu.HBM), pl.BlockSpec(memory_space=pltpu.VMEM)
    return pl.pallas_call(
        load_kernel,
        out_shape=[pltpu.VMEM(w.shape, w.dtype) for w in (wq, wkv, wo)],
        in_specs=[hbm] * 3,
        out_specs=[vmem] * 3,
        scratch_shapes=[pltpu.SemaphoreType.DMA((3,))],
        compiler_params=pltpu.CompilerParams(vmem_limit_bytes=2 * 1024 * 1024),
    )(wq, wkv, wo)


def combine_kernel(where, own, other, base, local, out):
    first, entry = where[0] == 0, where[0] < 2
    for slot in range(2):
        moved = own[slot].astype(f32) + other[1 - slot].astype(f32)
        fresh = local[...] if slot == 0 else own[0]
        moved = jnp.where(entry, fresh, moved.astype(bf16)).astype(f32)
        out[slot] = jnp.where(first, moved, base[slot].astype(f32) + moved).astype(bf16)


def combine(where, own, other, base, local):
    vmem = pl.BlockSpec(memory_space=pltpu.VMEM)
    return pl.pallas_call(
        combine_kernel,
        out_shape=jax.ShapeDtypeStruct(own.shape, own.dtype),
        in_specs=[pl.BlockSpec(memory_space=pltpu.SMEM)] + [vmem] * 4,
        out_specs=vmem,
        compiler_params=pltpu.CompilerParams(vmem_limit_bytes=4 * 1024 * 1024),
    )(where, own, other, base, local)


def body(
    stream_two, block_last, incoming_two, incoming_last, norm_gain,
    w_query, w_keyval, w_out, keys_cache, values_cache, cached_len,
):
    sections = lax.axis_size("section")
    tensors = lax.axis_size("tensor")
    sid = lax.axis_index("section")
    tid = lax.axis_index("tensor")
    rows = stream_two.shape[1]
    send = functools.partial(lambda v, f: move(v, sections, tensors, f))
    last = sections - 1
    first, final = sid == 0, sid == last

    def after(value, *others):
        return lax.optimization_barrier((value, others))[0]

    def exchange(parts):
        return [parts[0]] + [send(parts[k], y_shift(k)) for k in ORDER]

    def gather(pair):
        return exchange([pair] * Y)

    def add(a, b):
        return (a.astype(f32) + b.astype(f32)).astype(bf16)

    def halves(got):
        both = sum(g.astype(f32) for g in got)
        return both[0], both[1].astype(bf16)

    x0 = stream_two[0]
    pair0 = jnp.stack([x0, send(x0, hop(0, True))])
    wq = pltpu.with_memory_space_constraint(w_query[0], pltpu.HBM)
    wo = pltpu.with_memory_space_constraint(w_out[0], pltpu.HBM)

    ticks = keys_cache.shape[1]
    lengths = lax.dynamic_slice_in_dim(cached_len, last - sid, ticks)
    scalars = jnp.concatenate([lengths, jnp.stack([tid // Y, tid % Y]).astype(jnp.int32)])
    cos, sin = rope_tables(lengths, rows)
    wkv = w_keyval[0].reshape(w_keyval.shape[1], -1)

    pair0, scalars, cos, sin, wkv = lax.optimization_barrier(
        (pair0, scalars, cos, sin, wkv)
    )
    all0 = gather(pair0)
    wkv = pltpu.with_memory_space_constraint(wkv, pltpu.HBM)

    held = load(wq, wkv, wo)

    def block(tick, gathered, weights=None):
        return attend(
            tick, weights is not None, scalars, gathered, norm_gain, cos, sin,
            *(weights or (wq, wkv, wo)), keys_cache, values_cache,
        )

    early = after(block_last, all0[1])
    other1 = jnp.where(final, incoming_two[0], add(x0, early[0]))
    z1 = send(other1, hop(1, True))

    parts0 = block(0, all0, held)
    got0 = exchange(parts0)
    own1, enter_two, enter_last = after((other1, incoming_two, incoming_last), parts0)
    a1 = send(own1, hop(1))
    local = jnp.where(first, enter_two[1], enter_last[0])
    entering = jnp.where(final, enter_last[0], enter_two[1])
    got0, local, entering, a1 = lax.optimization_barrier((got0, local, entering, a1))
    sums0 = sum(g.astype(f32) for g in got0).astype(bf16)
    out2 = jnp.where(sid >= last - 1, entering[None], sums0)
    own, other = send(out2, hop(2)), send(out2, hop(2, True))
    a1, z1 = after((a1, z1), own)
    a1 = jnp.where(first, incoming_two[0], a1)
    pair1 = jnp.stack([a1, z1])
    base = send(pair1, hop(1))
    all1 = gather(pair1)
    pair2 = combine(sid.astype(jnp.int32)[None], own, other, base, local)
    all2 = gather(pair2)
    parts1 = block(1, after(all1, pair2))
    got1 = exchange(parts1)
    parts2 = block(2, after(all2, parts1))
    sums0, got1 = after((sums0, got1), parts2)
    got2 = lax.optimization_barrier(exchange(parts2))
    mine2, theirs2 = halves(got2)

    swapped0 = send(sums0[1], hop(0, True))
    mine1, theirs1 = halves(got1)
    swapped1 = send(theirs1, hop(0, True))
    swapped0, swapped1 = after((swapped0, swapped1), theirs2)
    b0 = add(sums0[0], swapped0)
    b1 = (mine1 + swapped1.astype(f32)).astype(bf16)
    s0 = add(x0, block_last[0])
    back = send(jnp.stack([b0, b1]), hop(1))
    t1 = add(a1, jnp.where(first, incoming_last[0], back[0]))
    t2 = add(pair2[0], jnp.where(first, incoming_last[1], back[1]))
    b2 = (mine2 + send(theirs2, hop(0, True)).astype(f32)).astype(bf16)
    return jnp.stack([s0, t1, t2])[None], jnp.stack([b0, b1, b2])[None]


def solution(mesh):
    placed = (
        P("section", None, "tensor"),
        P("section", None, "tensor"),
        P(None, None, "tensor"),
        P(None, None, "tensor"),
        P("section", None),
        P("section", None, "tensor"),
        P("section", None, None, "tensor"),
        P("section", "tensor", None),
        P("section", None, None, "tensor"),
        P("section", None, None, "tensor"),
        P(),
    )
    out = P("section", None, None, "tensor")
    return jax.shard_map(
        body, mesh=mesh, in_specs=placed, out_specs=(out, out), check_vma=False
    )
```
